256 devices in a mesh: outer: 16 (over z_lo, y, core), inner: 16 (over z_hi, x).
Axes of the slice: x: 4, y: 4, z: 8 (z_hi: 4, z_lo: 2; z = z_hi * 2 + z_lo), core: 2. Of those that a mesh axis runs over, the one named last changes fastest.
Arguments:
- queries: bfloat16 [65536, 4096], P(('outer', 'inner')), may hold values from -300 to 300
- key_codes: bfloat16 [65536, 1024], P(('outer', 'inner')), may hold values from -6 to 6
- value_code_rows: bfloat16 [65536, 1024], P(('outer', 'inner')), may hold values from -6 to 6
- key_span_scales: float32 [512, 8], P(('outer', 'inner')), may hold values from 0.5 to 2
- value_span_scales: float32 [512, 8], P(('outer', 'inner')), may hold values from 0.5 to 2
- formats: int32 [2, 8], replicated, may hold values from 0 to 1
- span_order: int32 [512], replicated, may hold values from 0 to 511, each once
Outputs:
- attended: bfloat16 [65536, 4096], P(('outer', 'inner'))
The draws below stay inside these ranges and needn't reach their ends.
Inputs may be any that keep to these rules, and one draw needn't show every extreme that they name: `span_order`: each span number appears once.
All inputs are finite; a program needn't handle non-finite values.
Results may differ from the reference program's by a relative error of at most 0.035.
Values may be sent and summed in bfloat16 or wider, within the bound.
A program may use at most 64 MiB of HBM per device.

```python
import math
import jax
import jax.numpy as jnp
from jax import lax

QUERY_HEADS = 32
KEY_HEADS = 8
HEAD_SIZE = 128
BLOCK_TOKENS = 256
SPAN_TOKENS = 128
GROUP_QUERIES = 4
SPAN_COUNT = 512
TOKEN_COUNT = 65536
N_OUTER = 16
N_INNER = 16


def shared_codes(key):
    return jnp.clip(jax.random.normal(key, (TOKEN_COUNT, KEY_HEADS * HEAD_SIZE), jnp.float32), -6.0, 6.0)


def draw_key_codes(key, part):
    base_offset = shared_codes(key)
    return base_offset.astype(jnp.bfloat16)


def draw_queries(key, part):
    key = jax.random.fold_in(key, 23)
    drawn = jnp.clip(jax.random.normal(key, (TOKEN_COUNT, QUERY_HEADS * HEAD_SIZE), jnp.float32), -6.0, 6.0)
    return drawn.astype(jnp.bfloat16)


def touch_ends(entries, key, low, top_value):
    shape = entries.shape
    spot = [jax.random.randint(jax.random.fold_in(key, axis), (), 0, shape[axis]) for axis in range(len(shape))]
    entries = entries.at[tuple(spot)].set(low)
    longest = shape.index(max(shape))
    spot[longest] = (spot[longest] + 1) % shape[longest]
    return entries.at[tuple(spot)].set(top_value)


def steps_of(stream_key, extent, cuts, smallest, top_value):
    def one(dim, shards_of):
        draws = jax.random.uniform(jax.random.fold_in(jax.random.fold_in(stream_key, 6), dim), (shards_of,), jnp.float32, smallest / len(cuts), top_value / len(cuts))
        return jnp.repeat(jnp.exp(draws), extent[dim] // shards_of).reshape((-1,) + (1,) * (len(extent) - dim - 1))

    level = one(*cuts[0])
    for cut in cuts[1:]:
        level = level * one(*cut)
    return level


def normal_values(own_key, dims, scale, bound, pieces=(), kind=jnp.bfloat16):
    result = jax.random.normal(own_key, dims, jnp.float32) * scale
    if len(pieces) > 0:
        result = steps_of(own_key, dims, pieces, -0.22, 0.18) * result
    return jnp.clip(result, min=-bound, max=bound).astype(kind)


def setup_inputs(seed: int = 0) -> dict:
    key_list = jax.random.split(jax.random.key(seed), 8)
    queries = draw_queries(jax.random.fold_in(key_list[7], 71), 0)
    key_codes = draw_key_codes(jax.random.fold_in(key_list[7], 71), 0)
    value_code_rows = normal_values(key_list[2], (TOKEN_COUNT, KEY_HEADS * HEAD_SIZE), 1.0, 6.0, ((0, 256),))
    key_span_scales = jnp.clip(jnp.exp(math.log(2.0) - 1.3862944 * jax.random.uniform(key_list[3], (SPAN_COUNT, KEY_HEADS), jnp.float32) ** steps_of(key_list[3], (SPAN_COUNT, KEY_HEADS), ((0, 256),), -0.2, 0.2)), 0.5, 2.0)
    value_span_scales = jnp.clip(jnp.exp(math.log(2.0) - 1.3862944 * jax.random.uniform(key_list[4], (SPAN_COUNT, KEY_HEADS), jnp.float32) ** steps_of(key_list[4], (SPAN_COUNT, KEY_HEADS), ((0, 256),), -0.2, 0.2)), 0.5, 2.0)
    formats = touch_ends(jax.random.randint(key_list[5], (2, KEY_HEADS), 0, 2), jax.random.fold_in(key_list[5], 1), 0, 1).astype(jnp.int32)
    span_order = jax.random.permutation(key_list[6], SPAN_COUNT).astype(jnp.int32)
    return dict(queries=queries, key_codes=key_codes, value_code_rows=value_code_rows, key_span_scales=key_span_scales, value_span_scales=value_span_scales, formats=formats, span_order=span_order)


def dequantize(code_matrix, scales, units):
    reshaped_rows = code_matrix.reshape(SPAN_COUNT, SPAN_TOKENS, KEY_HEADS, HEAD_SIZE).astype(jnp.float32)
    reshaped_rows = reshaped_rows * scales[:, None, :, None] * units[None, None, :, None]
    return reshaped_rows.astype(jnp.bfloat16).reshape(TOKEN_COUNT, KEY_HEADS, HEAD_SIZE)

def reference(queries, key_codes, value_code_rows, key_span_scales, value_span_scales, formats, span_order):
    units = jnp.where(formats == 0, 1.0, 0.25).astype(jnp.float32)
    key_deq = dequantize(key_codes, key_span_scales, units[0])
    value_deq = dequantize(value_code_rows, value_span_scales, units[1])
    offsets = jnp.arange(SPAN_TOKENS, dtype=jnp.int32)
    positions = (span_order[:, None].astype(jnp.int32) * SPAN_TOKENS + offsets[None, :]).reshape(TOKEN_COUNT).astype(jnp.int32)
    factor = 1.0 / math.sqrt(HEAD_SIZE)

    def one_block(block):
        outer_idx = block // N_INNER
        inner_idx = block % N_INNER
        key_rows, value_rows, key_pos = ([], [], [])
        for down_outer in range(2):
            for down_inner in range(3):
                source = (outer_idx - down_outer) % N_OUTER * N_INNER + (inner_idx - down_inner) % N_INNER
                start = (source * BLOCK_TOKENS).astype(jnp.int32)
                key_rows.append(lax.dynamic_slice_in_dim(key_deq, start, BLOCK_TOKENS, 0))
                value_rows.append(lax.dynamic_slice_in_dim(value_deq, start, BLOCK_TOKENS, 0))
                key_pos.append(lax.dynamic_slice_in_dim(positions, start, BLOCK_TOKENS, 0))
        keys = jnp.concatenate(key_rows, 0).astype(jnp.float32)
        values = jnp.concatenate(value_rows, 0).astype(jnp.float32)
        kpos = jnp.concatenate(key_pos, 0)
        qstart = (block * BLOCK_TOKENS).astype(jnp.int32)
        query_rows = lax.dynamic_slice_in_dim(queries, qstart, BLOCK_TOKENS, 0)
        qpos = lax.dynamic_slice_in_dim(positions, qstart, BLOCK_TOKENS, 0)
        query_head = query_rows.reshape(BLOCK_TOKENS, KEY_HEADS, GROUP_QUERIES, HEAD_SIZE).astype(jnp.float32)
        score = jnp.einsum('tkgd,ckd->kgtc', query_head, keys) * factor
        allowed = (kpos[None, :] <= qpos[:, None])[None, None]
        masked = jnp.where(allowed, score, -jnp.inf)
        peak = lax.optimization_barrier(jnp.max(masked, axis=-1, keepdims=True))
        expo = jnp.where(allowed, jnp.exp(masked - peak), 0.0)
        total = lax.optimization_barrier(jnp.sum(expo, axis=-1))
        weights = expo.astype(jnp.bfloat16).astype(jnp.float32)
        summed = jnp.einsum('kgtc,ckd->kgtd', weights, values) / total[..., None]
        return summed.transpose(2, 0, 1, 3).reshape(BLOCK_TOKENS, QUERY_HEADS * HEAD_SIZE).astype(jnp.bfloat16)
    blocks = jnp.arange(N_OUTER * N_INNER, dtype=jnp.int32)
    return lax.map(one_block, blocks).reshape(TOKEN_COUNT, QUERY_HEADS * HEAD_SIZE)
```

```python
import math

import jax
import jax.numpy as jnp
from jax import lax
from jax.experimental import pallas as pl
from jax.experimental.pallas import tpu as pltpu
from jax.sharding import PartitionSpec as P

MESH = pl.DeviceIdType.MESH
KEY_HEADS = 8
GROUP = 4
SIZE = 128
SPAN = 128
ROWS = 256
SLOTS = 6
EXP_SCALE = math.log2(math.e) / math.sqrt(SIZE)

OWN, IN1, IN2, OUT0, OUT1, OUT2, VIA_Z, VIA_X, VIA_Y = range(9)
F_IN1, F_DOWN, F_OUT0, F_WRAP, F_DOWN2, F_UP2, F_OUT1, F_OUT2, F_YWRAP = range(9)

UP_HEADS = 3
FIRST_HEADS = (5, 6)
AHEAD = 1
LEADS = (0, 1, 1, 2, 3, 4, 5)


def kernel(
    kscale, vscale, formats, order, k_ref, v_ref, q_hbm, out_hbm,
    kv, bias, q_ref, o_ref, recv, sent, q_sem, o_sem,
):
    o = lax.axis_index("outer")
    i = lax.axis_index("inner")
    c = o % 2
    y = (o // 2) % 4
    x = i % 4
    zh = i // 4

    def swapped(h):
        return (h * 3) % KEY_HEADS

    def up(h):
        return swapped(h) < UP_HEADS

    def x_first(h):
        return swapped(h) < jnp.where(c == 0, FIRST_HEADS[0], FIRST_HEADS[1])

    next_in = (i + 1) % 16
    next_out = (o + 1) % 16
    source_x = (x + 1) % 4
    down_to = zh * 4 + (x + 3) % 4
    down2_to = (zh * 4 + source_x + 2) % 16
    wraps_y = o == 7

    q_copy = pltpu.make_async_copy(q_hbm, q_ref, q_sem)
    q_copy.start()

    barrier = pltpu.get_barrier_semaphore()

    def greet(outer, inner):
        pl.semaphore_signal(barrier, inc=1, device_id=(outer, inner), device_id_type=MESH)

    greet(o, (i + 15) % 16)
    greet(o, zh * 4 + (x + 1) % 4)
    two_back = (i + 14) % 16
    greet(o, (two_back // 4) * 4 + (x + 1) % 4)
    greet((o + 15) % 16, i)

    @pl.when(x == 0)
    def _():
        greet(o, i + 3)
        greet(o, (i + 12) % 16)

    @pl.when(jnp.logical_or(o == 1, o == 3))
    def _():
        greet(7, i)

    @pl.when(o == 8)
    def _():
        greet(1, i)
        greet(3, i)

    for h in range(KEY_HEADS):
        for which, codes, scale in ((0, k_ref, kscale), (1, v_ref, vscale)):
            unit = jnp.where(formats[which, h] == 0, 1.0, 0.25)
            for s in range(2):
                rows = pl.ds(s * SPAN, SPAN)
                part = codes[rows, h * SIZE:(h + 1) * SIZE].astype(jnp.float32)
                kv[h, OWN, which, rows] = (part * (scale[s, h] * unit)).astype(jnp.bfloat16)

    peers = (
        4
        + jnp.where(jnp.logical_or(x == 0, x == 3), 1, 0)
        + jnp.where(jnp.logical_or(o == 1, o == 3), 1, 0)
        + jnp.where(wraps_y, 2, 0)
    )
    pl.semaphore_wait(barrier, peers)

    def send(h, source, target, flow, device):
        pltpu.make_async_remote_copy(
            kv.at[h, source], kv.at[h, target], sent.at[h, flow], recv.at[h, target],
            device_id=device, device_id_type=MESH,
        ).start()

    def arrived(h, slot):
        pltpu.make_async_copy(kv.at[h, slot], kv.at[h, slot], recv.at[h, slot]).wait()

    def left(h, flow):
        pltpu.make_async_copy(kv.at[h, OWN], kv.at[h, OWN], sent.at[h, flow]).wait()

    def send_own(h):
        round_x = jnp.logical_and(x == 3, x_first(h))

        @pl.when(round_x)
        def _():
            send(h, OWN, VIA_Z, F_IN1, (o, i - 3))

        @pl.when(jnp.logical_not(round_x))
        def _():
            send(h, OWN, IN1, F_IN1, (o, next_in))

        @pl.when(jnp.logical_not(up(h)))
        def _():
            send(h, OWN, VIA_X, F_DOWN, (o, down_to))

        send(h, OWN, OUT0, F_OUT0, (next_out, i))

    def relay_wrap(h):
        @pl.when(jnp.logical_and(x == 0, x_first(h)))
        def _():
            arrived(h, VIA_Z)
            send(h, VIA_Z, IN1, F_WRAP, (o, (i + 4) % 16))

    def relay_down(h):
        @pl.when(jnp.logical_not(up(h)))
        def _():
            arrived(h, VIA_X)
            send(h, VIA_X, IN2, F_DOWN2, (o, down2_to))

    def relay_in1(h):
        arrived(h, IN1)

        @pl.when(up(h))
        def _():
            send(h, IN1, IN2, F_UP2, (o, next_in))

        @pl.when(wraps_y)
        def _():
            send(h, IN1, VIA_Y, F_OUT1, (1, i))

        @pl.when(jnp.logical_not(wraps_y))
        def _():
            send(h, IN1, OUT1, F_OUT1, (next_out, i))

    def relay_in2(h):
        arrived(h, IN2)

        @pl.when(wraps_y)
        def _():
            send(h, IN2, VIA_Y, F_OUT2, (3, i))

        @pl.when(jnp.logical_not(wraps_y))
        def _():
            send(h, IN2, OUT2, F_OUT2, (next_out, i))

    def relay_y(h):
        @pl.when(o == 1)
        def _():
            arrived(h, VIA_Y)
            send(h, VIA_Y, OUT1, F_YWRAP, (8, i))

        @pl.when(o == 3)
        def _():
            arrived(h, VIA_Y)
            send(h, VIA_Y, OUT2, F_YWRAP, (8, i))

    def out_copy(h):
        return pltpu.make_async_copy(
            o_ref.at[h],
            out_hbm.at[:, pl.ds(pl.multiple_of(h * (GROUP * SIZE), GROUP * SIZE), GROUP * SIZE)],
            o_sem.at[h],
        )

    def attend(h):
        arrived(h, OUT0)
        arrived(h, OUT1)
        arrived(h, OUT2)

        @pl.when(h == 0)
        def _():
            q_copy.wait()

        for g in range(GROUP):
            columns = pl.ds(pl.multiple_of((h * GROUP + g) * SIZE, SIZE), SIZE)
            keys = kv[h, 0:SLOTS, 0].reshape(SLOTS * ROWS, SIZE)
            values = kv[h, 0:SLOTS, 1].reshape(SLOTS * ROWS, SIZE)
            score = lax.dot_general(
                q_ref[:, columns], keys, (((1,), (1,)), ((), ())),
                preferred_element_type=jnp.float32,
            ) + bias[...]
            peak = jnp.max(score, axis=1, keepdims=True)
            expo = jnp.exp2((score - peak) * EXP_SCALE)
            total = jnp.sum(expo, axis=1, keepdims=True)
            summed = jnp.dot(expo.astype(jnp.bfloat16), values, preferred_element_type=jnp.float32)
            o_ref[h, :, g * SIZE:(g + 1) * SIZE] = (summed / total).astype(jnp.bfloat16)
        out_copy(h).start()

    stages = (send_own, relay_wrap, relay_down, relay_in1, relay_in2, relay_y, attend)

    def first(h, carry):
        send_own(h)
        return carry

    def step(t, carry):
        for stage, lead in zip(stages, LEADS):
            h = t - lead + (AHEAD if stage is send_own else 0)

            @pl.when(jnp.logical_and(h >= 0, h < KEY_HEADS))
            def _():
                stage(h)

        return carry

    lax.fori_loop(0, AHEAD, first, 0)

    below = lax.broadcasted_iota(jnp.int32, (SPAN, SPAN), 0)
    across = lax.broadcasted_iota(jnp.int32, (SPAN, SPAN), 1)
    for slot, (d_out, d_in) in enumerate(((0, 0), (0, 1), (0, 2), (1, 0), (1, 1), (1, 2))):
        block = ((o + 16 - d_out) % 16) * 16 + (i + 16 - d_in) % 16
        for s in range(2):
            key_at = order[block * 2 + s] * SPAN
            for r in range(2):
                query_at = order[(o * 16 + i) * 2 + r] * SPAN
                seen = key_at + across <= query_at + below
                bias[r * SPAN:(r + 1) * SPAN, (slot * 2 + s) * SPAN:(slot * 2 + s + 1) * SPAN] = (
                    jnp.where(seen, 0.0, -jnp.inf)
                )

    lax.fori_loop(0, KEY_HEADS + LEADS[-1], step, 0)

    def finish(h, carry):
        out_copy(h).wait()
        for flow in (F_IN1, F_OUT0, F_OUT1, F_OUT2):
            left(h, flow)

        @pl.when(up(h))
        def _():
            left(h, F_UP2)

        @pl.when(jnp.logical_not(up(h)))
        def _():
            left(h, F_DOWN)
            left(h, F_DOWN2)

        @pl.when(jnp.logical_and(x == 0, x_first(h)))
        def _():
            left(h, F_WRAP)

        @pl.when(jnp.logical_or(o == 1, o == 3))
        def _():
            left(h, F_YWRAP)

        return carry

    lax.fori_loop(0, KEY_HEADS, finish, 0)


def shards(queries, key_codes, value_code_rows, key_scales, value_scales, formats, span_order):
    vmem = pl.BlockSpec(memory_space=pltpu.VMEM)
    smem = pl.BlockSpec(memory_space=pltpu.SMEM)
    anywhere = pl.BlockSpec(memory_space=pl.ANY)
    flops = 4 * 32 * ROWS * SLOTS * ROWS * SIZE
    return pl.pallas_call(
        kernel,
        out_shape=jax.ShapeDtypeStruct((ROWS, KEY_HEADS * GROUP * SIZE), jnp.bfloat16),
        in_specs=[smem, smem, smem, smem, vmem, vmem, anywhere],
        out_specs=anywhere,
        scratch_shapes=[
            pltpu.VMEM((KEY_HEADS, 9, 2, ROWS, SIZE), jnp.bfloat16),
            pltpu.VMEM((ROWS, SLOTS * ROWS), jnp.float32),
            pltpu.VMEM((ROWS, KEY_HEADS * GROUP * SIZE), jnp.bfloat16),
            pltpu.VMEM((KEY_HEADS, ROWS, GROUP * SIZE), jnp.bfloat16),
            pltpu.SemaphoreType.DMA((KEY_HEADS, 9)),
            pltpu.SemaphoreType.DMA((KEY_HEADS, 9)),
            pltpu.SemaphoreType.DMA,
            pltpu.SemaphoreType.DMA((KEY_HEADS,)),
        ],
        compiler_params=pltpu.CompilerParams(
            collective_id=1, has_side_effects=True, vmem_limit_bytes=48 * 2**20
        ),
        cost_estimate=pl.CostEstimate(
            flops=flops, bytes_accessed=6 * 2**20, transcendentals=32 * ROWS * SLOTS * ROWS
        ),
        name="block_window_attention",
    )(key_scales, value_scales, formats, span_order, key_codes, value_code_rows, queries)


def solution(mesh):
    split = P(("outer", "inner"), None)
    return jax.shard_map(
        shards,
        mesh=mesh,
        in_specs=(split, split, split, split, split, P(), P()),
        out_specs=split,
        check_vma=False,
    )
```

```python
import math

import jax
import jax.numpy as jnp
from jax import lax
from jax.experimental import pallas as pl
from jax.experimental.pallas import tpu as pltpu
from jax.sharding import PartitionSpec as P

MESH = pl.DeviceIdType.MESH
KEY_HEADS = 8
GROUP = 4
SIZE = 128
SPAN = 128
ROWS = 256
SLOTS = 6
HALF = 3
EXP_SCALE = math.log2(math.e) / math.sqrt(SIZE)

OWN, OUT0, IN1, IN2, OUT1, OUT2, VIA_Z, VIA_X, VIA_Y = range(9)
F_IN1, F_DOWN, F_OUT0, F_WRAP, F_DOWN2, F_UP2, F_OUT1, F_OUT2, F_YWRAP = range(9)

UP = (128, 256, 80, 352)
HIGH = 384
FIRST = 304
BOTH = 2 * ROWS


def plan_of(
    send_in, send_out, relay_wrap, relay_down, relay_in1, relay_in2, relay_y0, relay_y,
    attend_near, attend_far
):
    return (
        (send_in, -1),
        (relay_wrap, 1),
        (relay_y0, 1),
        (relay_down, 1),
        (relay_in1, 2),
        (relay_in2, 3),
        (relay_y, 3),
        (send_out, -1),
        (attend_near(range(GROUP)), 3),
        (attend_far(range(GROUP)), 4),
    )


def kernel(
    kscale, vscale, formats, order, k_hbm, v_hbm, q_hbm, out_hbm,
    kv, bias, sums, peaks, totals, k_ref, v_ref, q_ref, o_ref, recv, sent, in_sem, o_sem,
):
    o = lax.axis_index("outer")
    i = lax.axis_index("inner")
    c = o % 2
    y = (o // 2) % 4
    x = i % 4
    zh = i // 4

    next_in = (i + 1) % 16
    next_out = (o + 1) % 16
    source_x = (x + 1) % 4
    down_x = (x + 3) % 4
    down_to = zh * 4 + down_x
    down2_to = (zh * 4 + source_x + 2) % 16
    z_lo = o // 8
    wraps_y = jnp.logical_and(y == 3, c == 1)
    turns_y = jnp.logical_and(y < 2, c == 1)
    past_wrap = 8 - 8 * z_lo

    k_copy = pltpu.make_async_copy(k_hbm, k_ref, in_sem.at[0])
    v_copy = pltpu.make_async_copy(v_hbm, v_ref, in_sem.at[1])
    q_copy = pltpu.make_async_copy(q_hbm, q_ref, in_sem.at[2])
    k_copy.start()
    v_copy.start()
    q_copy.start()

    barrier = pltpu.get_barrier_semaphore()

    def greet(outer, inner):
        pl.semaphore_signal(barrier, inc=1, device_id=(outer, inner), device_id_type=MESH)

    greet(o, (i + 15) % 16)
    greet(o, zh * 4 + (x + 1) % 4)
    two_back = (i + 14) % 16
    greet(o, (two_back // 4) * 4 + (x + 1) % 4)
    greet((o + 15) % 16, i)

    @pl.when(x == 0)
    def _():
        greet(o, i + 3)
        greet(o, (i + 12) % 16)

    @pl.when(x == 1)
    def _():
        greet(o, (i + 13) % 16)

    @pl.when(turns_y)
    def _():
        greet(z_lo * 8 + 7, i)

    @pl.when(jnp.logical_and(y == 0, c == 0))
    def _():
        greet(past_wrap + 1, i)
        greet(past_wrap + 3, i)

    for which, codes, scale, copy in ((0, k_ref, kscale, k_copy), (1, v_ref, vscale, v_copy)):
        copy.wait()
        for h in range(KEY_HEADS):
            unit = jnp.where(formats[which, h] == 0, 1.0, 0.25)
            for s in range(2):
                part = codes[s * SPAN:(s + 1) * SPAN, h * SIZE:(h + 1) * SIZE].astype(jnp.float32)
                start = which * ROWS + s * SPAN
                kv[h, OWN, start:start + SPAN] = (part * (scale[s, h] * unit)).astype(jnp.bfloat16)

    peers = (
        4
        + jnp.where(jnp.logical_or(x == 0, x == 3), 1, 0)
        + jnp.where(turns_y, 1, 0)
        + jnp.where(x == 2, 1, 0)
        + jnp.where(wraps_y, 2, 0)
    )
    pl.semaphore_wait(barrier, peers)

    def send(h, source, target, flow, device, start=0, stop=BOTH):
        rows = pl.ds(start, stop - start)
        pltpu.make_async_remote_copy(
            kv.at[h, source, rows], kv.at[h, target, rows], sent.at[h, flow], recv.at[h, target],
            device_id=device, device_id_type=MESH,
        ).start()

    def arrived(h, slot, start=0, stop=BOTH):
        rows = pl.ds(start, stop - start)
        pltpu.make_async_copy(kv.at[h, slot, rows], kv.at[h, slot, rows], recv.at[h, slot]).wait()

    def left(h, flow, start=0, stop=BOTH):
        rows = pl.ds(start, stop - start)
        pltpu.make_async_copy(kv.at[h, OWN, rows], kv.at[h, OWN, rows], sent.at[h, flow]).wait()

    def send_in(h):
        @pl.when(x == 3)
        def _():
            send(h, OWN, VIA_Z, F_IN1, (o, i - 3), 0, FIRST)
            send(h, OWN, IN1, F_IN1, (o, next_in), FIRST, BOTH)

        @pl.when(x != 3)
        def _():
            send(h, OWN, IN1, F_IN1, (o, next_in))

        for at in range(4):
            @pl.when(x == at)
            def _():
                stop = HIGH if at == 2 else BOTH
                send(h, OWN, VIA_X, F_DOWN, (o, down_to), UP[at], stop)
                if at == 2:
                    send(h, OWN, VIA_X, F_DOWN, (o, (i + 3) % 16), HIGH, BOTH)

    def send_out(h):
        @pl.when(wraps_y)
        def _():
            send(h, OWN, VIA_Y, F_OUT0, (z_lo * 8 + 3, i))

        @pl.when(jnp.logical_not(wraps_y))
        def _():
            send(h, OWN, OUT0, F_OUT0, (next_out, i))

    def relay_wrap(h):
        @pl.when(x == 0)
        def _():
            arrived(h, VIA_Z, 0, FIRST)
            send(h, VIA_Z, IN1, F_WRAP, (o, (i + 4) % 16), 0, FIRST)

    def relay_down(h):
        for at in range(4):
            @pl.when(source_x == at)
            def _():
                stop = HIGH if at == 2 else BOTH
                arrived(h, VIA_X, UP[at], BOTH)
                send(h, VIA_X, IN2, F_DOWN2, (o, down2_to), UP[at], stop)
                if at == 2:
                    send(h, VIA_X, IN2, F_DOWN2, (o, i - 1), HIGH, BOTH)

    def relay_in1(h):
        arrived(h, IN1)
        for at in range(4):
            @pl.when(down_x == at)
            def _():
                send(h, IN1, IN2, F_UP2, (o, next_in), 0, UP[at])

        @pl.when(wraps_y)
        def _():
            send(h, IN1, VIA_Y, F_OUT1, (z_lo * 8 + 1, i))

        @pl.when(jnp.logical_not(wraps_y))
        def _():
            send(h, IN1, OUT1, F_OUT1, (next_out, i))

    def relay_in2(h):
        arrived(h, IN2)
        send(h, IN2, OUT2, F_OUT2, (next_out, i))

    def relay_y(h):
        @pl.when(jnp.logical_and(y == 0, c == 1))
        def _():
            arrived(h, VIA_Y)
            send(h, VIA_Y, OUT1, F_YWRAP, (past_wrap, i))

    def relay_y0(h):
        @pl.when(jnp.logical_and(y == 1, c == 1))
        def _():
            arrived(h, VIA_Y)
            send(h, VIA_Y, OUT0, F_YWRAP, (past_wrap, i))

    def out_copy(h):
        return pltpu.make_async_copy(
            o_ref.at[h],
            out_hbm.at[:, pl.ds(pl.multiple_of(h * (GROUP * SIZE), GROUP * SIZE), GROUP * SIZE)],
            o_sem.at[h],
        )

    def scores(h, g, first):
        columns = pl.ds(pl.multiple_of((h * GROUP + g) * SIZE, SIZE), SIZE)
        keys = kv[h, first:first + HALF, 0:ROWS].reshape(HALF * ROWS, SIZE)
        return lax.dot_general(
            q_ref[:, columns], keys, (((1,), (1,)), ((), ())),
            preferred_element_type=jnp.float32,
        ) + bias[:, first * ROWS:(first + HALF) * ROWS]

    def weighted(h, score, peak, first):
        expo = jnp.exp2((score - peak) * EXP_SCALE)
        values = kv[h, first:first + HALF, ROWS:BOTH].reshape(HALF * ROWS, SIZE)
        values = jnp.concatenate([values, jnp.ones((HALF * ROWS, SIZE), jnp.bfloat16)], axis=1)
        summed = jnp.dot(expo.astype(jnp.bfloat16), values, preferred_element_type=jnp.float32)
        return summed[:, :SIZE], summed[:, SIZE:]

    def attend_near(gs):
        def run(h):
            arrived(h, OUT0)

            @pl.when(h == 0)
            def _():
                q_copy.wait()

            for g in gs:
                score = scores(h, g, 0)
                peak = jnp.max(score, axis=1, keepdims=True)
                summed, total = weighted(h, score, peak, 0)
                sums[h, g] = summed
                peaks[h, g] = jnp.broadcast_to(peak, (ROWS, SIZE))
                totals[h, g] = total

        return run

    def attend_far(gs):
        def run(h):
            arrived(h, OUT1)
            arrived(h, OUT2)
            for g in gs:
                score = scores(h, g, HALF)
                near = peaks[h, g][:, 0:1]
                peak = jnp.maximum(near, jnp.max(score, axis=1, keepdims=True))
                summed, total = weighted(h, score, peak, HALF)
                keep = jnp.exp2((near - peak) * EXP_SCALE)
                result = (sums[h, g] * keep + summed) / (totals[h, g] * keep + total)
                o_ref[h, :, g * SIZE:(g + 1) * SIZE] = result.astype(jnp.bfloat16)
            out_copy(h).start()

        return run

    plan = plan_of(
        send_in, send_out, relay_wrap, relay_down, relay_in1, relay_in2, relay_y0, relay_y,
        attend_near, attend_far,
    )
    end = KEY_HEADS + max(lead for _, lead in plan)
    send_in(0)
    send_out(0)

    def step(t, carry):
        for stage, lead in plan:
            h = t - lead

            @pl.when(jnp.logical_and(h >= 0, h < KEY_HEADS))
            def _():
                stage(h)

        return carry

    below = lax.broadcasted_iota(jnp.int32, (SPAN, SPAN), 0)
    across = lax.broadcasted_iota(jnp.int32, (SPAN, SPAN), 1)
    for slot, (d_out, d_in) in enumerate(((0, 0), (1, 0), (0, 1), (0, 2), (1, 1), (1, 2))):
        block = ((o + 16 - d_out) % 16) * 16 + (i + 16 - d_in) % 16
        for s in range(2):
            key_at = order[block * 2 + s] * SPAN
            for r in range(2):
                query_at = order[(o * 16 + i) * 2 + r] * SPAN
                seen = key_at + across <= query_at + below
                bias[r * SPAN:(r + 1) * SPAN, (slot * 2 + s) * SPAN:(slot * 2 + s + 1) * SPAN] = (
                    jnp.where(seen, 0.0, -jnp.inf)
                )

    lax.fori_loop(0, end, step, 0)

    def finish(h, carry):
        out_copy(h).wait()
        for flow in (F_IN1, F_OUT0, F_OUT1, F_OUT2):
            left(h, flow)
        for at in range(4):
            @pl.when(x == at)
            def _():
                left(h, F_DOWN, UP[at], BOTH)

            @pl.when(source_x == at)
            def _():
                left(h, F_DOWN2, UP[at], BOTH)

            @pl.when(down_x == at)
            def _():
                left(h, F_UP2, 0, UP[at])

        @pl.when(x == 0)
        def _():
            left(h, F_WRAP, 0, FIRST)

        @pl.when(turns_y)
        def _():
            left(h, F_YWRAP)

        return carry

    lax.fori_loop(0, KEY_HEADS, finish, 0)


def shards(queries, key_codes, value_code_rows, key_scales, value_scales, formats, span_order):
    smem = pl.BlockSpec(memory_space=pltpu.SMEM)
    anywhere = pl.BlockSpec(memory_space=pl.ANY)
    flops = 4 * 32 * ROWS * SLOTS * ROWS * SIZE
    return pl.pallas_call(
        kernel,
        out_shape=jax.ShapeDtypeStruct((ROWS, KEY_HEADS * GROUP * SIZE), jnp.bfloat16),
        in_specs=[smem, smem, smem, smem, anywhere, anywhere, anywhere],
        out_specs=anywhere,
        scratch_shapes=[
            pltpu.VMEM((KEY_HEADS, 9, BOTH, SIZE), jnp.bfloat16),
            pltpu.VMEM((ROWS, SLOTS * ROWS), jnp.float32),
            pltpu.VMEM((KEY_HEADS, GROUP, ROWS, SIZE), jnp.float32),
            pltpu.VMEM((KEY_HEADS, GROUP, ROWS, SIZE), jnp.float32),
            pltpu.VMEM((KEY_HEADS, GROUP, ROWS, SIZE), jnp.float32),
            pltpu.VMEM((ROWS, KEY_HEADS * SIZE), jnp.bfloat16),
            pltpu.VMEM((ROWS, KEY_HEADS * SIZE), jnp.bfloat16),
            pltpu.VMEM((ROWS, KEY_HEADS * GROUP * SIZE), jnp.bfloat16),
            pltpu.VMEM((KEY_HEADS, ROWS, GROUP * SIZE), jnp.bfloat16),
            pltpu.SemaphoreType.DMA((KEY_HEADS, 9)),
            pltpu.SemaphoreType.DMA((KEY_HEADS, 9)),
            pltpu.SemaphoreType.DMA((3,)),
            pltpu.SemaphoreType.DMA((KEY_HEADS,)),
        ],
        compiler_params=pltpu.CompilerParams(
            collective_id=1, has_side_effects=True, vmem_limit_bytes=60 * 2**20
        ),
        cost_estimate=pl.CostEstimate(
            flops=flops, bytes_accessed=6 * 2**20, transcendentals=32 * ROWS * SLOTS * ROWS
        ),
        name="block_window_attention",
    )(key_scales, value_scales, formats, span_order, key_codes, value_code_rows, queries)


def solution(mesh):
    split = P(("outer", "inner"), None)
    return jax.shard_map(
        shards,
        mesh=mesh,
        in_specs=(split, split, split, split, split, P(), P()),
        out_specs=split,
        check_vma=False,
    )
```

```python
import math

import jax
import jax.numpy as jnp
from jax import lax
from jax.experimental import pallas as pl
from jax.experimental.pallas import tpu as pltpu
from jax.sharding import PartitionSpec as P

MESH = pl.DeviceIdType.MESH
KEY_HEADS = 8
GROUP = 4
SIZE = 128
SPAN = 128
ROWS = 256
SLOTS = 6
HALF = 3
EXP_SCALE = math.log2(math.e) / math.sqrt(SIZE)

OWN, OUT0, IN1, IN2, OUT1, OUT2, VIA_Z, VIA_X, VIA_Y = range(9)
F_IN1, F_DOWN, F_OUT0, F_WRAP, F_DOWN2, F_UP2, F_OUT1, F_OUT2, F_YWRAP = range(9)

UP = (128, 256, 80, 352)
HIGH = 384
FIRST = 304
BOTH = 2 * ROWS


def plan_of(
    send_via, send_in, send_out, relay_wrap, relay_down, relay_in1, relay_in2, relay_y0, relay_y,
    attend_near, attend_far
):
    return (
        (send_via, -2),
        (send_in, -2),
        (relay_wrap, 1),
        (relay_down, 1),
        (relay_y0, 1),
        (relay_in1, 2),
        (relay_in2, 3),
        (relay_y, 3),
        (send_out, -1),
        (attend_near(range(GROUP)), 3),
        (attend_far(range(GROUP)), 4),
    )


def kernel(
    kscale, vscale, formats, order, k_hbm, v_hbm, q_hbm, out_hbm,
    kv, bias, sums, peaks, totals, k_ref, v_ref, q_ref, o_ref, recv, sent, in_sem, o_sem,
):
    o = lax.axis_index("outer")
    i = lax.axis_index("inner")
    c = o % 2
    y = (o // 2) % 4
    x = i % 4
    zh = i // 4

    next_in = (i + 1) % 16
    next_out = (o + 1) % 16
    source_x = (x + 1) % 4
    down_x = (x + 3) % 4
    down_to = zh * 4 + down_x
    down2_to = (zh * 4 + source_x + 2) % 16
    z_lo = o // 8
    wraps_y = jnp.logical_and(y == 3, c == 1)
    turns_y = jnp.logical_and(y < 2, c == 1)
    past_wrap = 8 - 8 * z_lo

    k_copy = pltpu.make_async_copy(k_hbm, k_ref, in_sem.at[0])
    v_copy = pltpu.make_async_copy(v_hbm, v_ref, in_sem.at[1])
    q_copy = pltpu.make_async_copy(q_hbm, q_ref, in_sem.at[2])
    k_copy.start()
    v_copy.start()
    q_copy.start()

    barrier = pltpu.get_barrier_semaphore()

    def greet(outer, inner):
        pl.semaphore_signal(barrier, inc=1, device_id=(outer, inner), device_id_type=MESH)

    greet(o, (i + 15) % 16)
    greet(o, zh * 4 + (x + 1) % 4)
    two_back = (i + 14) % 16
    greet(o, (two_back // 4) * 4 + (x + 1) % 4)
    greet((o + 15) % 16, i)

    @pl.when(x == 0)
    def _():
        greet(o, i + 3)
        greet(o, (i + 12) % 16)

    @pl.when(x == 1)
    def _():
        greet(o, (i + 13) % 16)

    @pl.when(turns_y)
    def _():
        greet(z_lo * 8 + 7, i)

    @pl.when(jnp.logical_and(y == 0, c == 0))
    def _():
        greet(past_wrap + 1, i)
        greet(past_wrap + 3, i)

    for which, codes, scale, copy in ((0, k_ref, kscale, k_copy), (1, v_ref, vscale, v_copy)):
        copy.wait()
        for h in range(KEY_HEADS):
            unit = jnp.where(formats[which, h] == 0, 1.0, 0.25)
            for s in range(2):
                part = codes[s * SPAN:(s + 1) * SPAN, h * SIZE:(h + 1) * SIZE].astype(jnp.float32)
                start = which * ROWS + s * SPAN
                kv[h, OWN, start:start + SPAN] = (part * (scale[s, h] * unit)).astype(jnp.bfloat16)

    peers = (
        4
        + jnp.where(jnp.logical_or(x == 0, x == 3), 1, 0)
        + jnp.where(turns_y, 1, 0)
        + jnp.where(x == 2, 1, 0)
        + jnp.where(wraps_y, 2, 0)
    )
    pl.semaphore_wait(barrier, peers)

    def send(h, source, target, flow, device, start=0, stop=BOTH):
        rows = pl.ds(start, stop - start)
        pltpu.make_async_remote_copy(
            kv.at[h, source, rows], kv.at[h, target, rows], sent.at[h, flow], recv.at[h, target],
            device_id=device, device_id_type=MESH,
        ).start()

    def arrived(h, slot, start=0, stop=BOTH):
        rows = pl.ds(start, stop - start)
        pltpu.make_async_copy(kv.at[h, slot, rows], kv.at[h, slot, rows], recv.at[h, slot]).wait()

    def left(h, flow, start=0, stop=BOTH):
        rows = pl.ds(start, stop - start)
        pltpu.make_async_copy(kv.at[h, OWN, rows], kv.at[h, OWN, rows], sent.at[h, flow]).wait()

    def send_via(h):
        @pl.when(x == 3)
        def _():
            send(h, OWN, VIA_Z, F_IN1, (o, i - 3), 0, FIRST)

        for at in range(4):
            @pl.when(x == at)
            def _():
                stop = HIGH if at == 2 else BOTH
                if at == 2:
                    send(h, OWN, VIA_X, F_DOWN, (o, (i + 3) % 16), HIGH, BOTH)
                send(h, OWN, VIA_X, F_DOWN, (o, down_to), UP[at], stop)

    def send_in(h):
        @pl.when(x == 3)
        def _():
            send(h, OWN, IN1, F_IN1, (o, next_in), FIRST, BOTH)

        @pl.when(x != 3)
        def _():
            send(h, OWN, IN1, F_IN1, (o, next_in))

    def send_out(h):
        @pl.when(wraps_y)
        def _():
            send(h, OWN, VIA_Y, F_OUT0, (z_lo * 8 + 3, i))

        @pl.when(jnp.logical_not(wraps_y))
        def _():
            send(h, OWN, OUT0, F_OUT0, (next_out, i))

    def relay_wrap(h):
        @pl.when(x == 0)
        def _():
            arrived(h, VIA_Z, 0, FIRST)
            send(h, VIA_Z, IN1, F_WRAP, (o, (i + 4) % 16), 0, FIRST)

    def relay_down(h):
        for at in range(4):
            @pl.when(source_x == at)
            def _():
                stop = HIGH if at == 2 else BOTH
                arrived(h, VIA_X, UP[at], BOTH)
                send(h, VIA_X, IN2, F_DOWN2, (o, down2_to), UP[at], stop)
                if at == 2:
                    send(h, VIA_X, IN2, F_DOWN2, (o, i - 1), HIGH, BOTH)

    def relay_in1(h):
        arrived(h, IN1)
        for at in range(4):
            @pl.when(down_x == at)
            def _():
                send(h, IN1, IN2, F_UP2, (o, next_in), 0, UP[at])

        @pl.when(wraps_y)
        def _():
            send(h, IN1, VIA_Y, F_OUT1, (z_lo * 8 + 1, i))

        @pl.when(jnp.logical_not(wraps_y))
        def _():
            send(h, IN1, OUT1, F_OUT1, (next_out, i))

    def relay_in2(h):
        arrived(h, IN2)
        send(h, IN2, OUT2, F_OUT2, (next_out, i))

    def relay_y(h):
        @pl.when(jnp.logical_and(y == 0, c == 1))
        def _():
            arrived(h, VIA_Y)
            send(h, VIA_Y, OUT1, F_YWRAP, (past_wrap, i))

    def relay_y0(h):
        @pl.when(jnp.logical_and(y == 1, c == 1))
        def _():
            arrived(h, VIA_Y)
            send(h, VIA_Y, OUT0, F_YWRAP, (past_wrap, i))

    def out_copy(h):
        return pltpu.make_async_copy(
            o_ref.at[h],
            out_hbm.at[:, pl.ds(pl.multiple_of(h * (GROUP * SIZE), GROUP * SIZE), GROUP * SIZE)],
            o_sem.at[h],
        )

    def scores(h, g, first):
        columns = pl.ds(pl.multiple_of((h * GROUP + g) * SIZE, SIZE), SIZE)
        keys = kv[h, first:first + HALF, 0:ROWS].reshape(HALF * ROWS, SIZE)
        return lax.dot_general(
            q_ref[:, columns], keys, (((1,), (1,)), ((), ())),
            preferred_element_type=jnp.float32,
        ) + bias[:, first * ROWS:(first + HALF) * ROWS]

    def weighted(h, score, peak, first):
        expo = jnp.exp2((score - peak) * EXP_SCALE)
        values = kv[h, first:first + HALF, ROWS:BOTH].reshape(HALF * ROWS, SIZE)
        values = jnp.concatenate([values, jnp.ones((HALF * ROWS, SIZE), jnp.bfloat16)], axis=1)
        summed = jnp.dot(expo.astype(jnp.bfloat16), values, preferred_element_type=jnp.float32)
        return summed[:, :SIZE], summed[:, SIZE:]

    def attend_near(gs):
        def run(h):
            arrived(h, OUT0)

            @pl.when(h == 0)
            def _():
                q_copy.wait()

            for g in gs:
                score = scores(h, g, 0)
                peak = jnp.max(score, axis=1, keepdims=True)
                summed, total = weighted(h, score, peak, 0)
                sums[h, g] = summed
                peaks[h, g] = jnp.broadcast_to(peak, (ROWS, SIZE))
                totals[h, g] = total

        return run

    def attend_far(gs):
        def run(h):
            arrived(h, OUT1)
            arrived(h, OUT2)
            for g in gs:
                score = scores(h, g, HALF)
                near = peaks[h, g][:, 0:1]
                peak = jnp.maximum(near, jnp.max(score, axis=1, keepdims=True))
                summed, total = weighted(h, score, peak, HALF)
                keep = jnp.exp2((near - peak) * EXP_SCALE)
                result = (sums[h, g] * keep + summed) / (totals[h, g] * keep + total)
                o_ref[h, :, g * SIZE:(g + 1) * SIZE] = result.astype(jnp.bfloat16)
            out_copy(h).start()

        return run

    plan = plan_of(
        send_via, send_in, send_out, relay_wrap, relay_down, relay_in1, relay_in2, relay_y0, relay_y,
        attend_near, attend_far,
    )
    end = KEY_HEADS + max(lead for _, lead in plan)
    for t in range(min(lead for _, lead in plan), 0):
        for stage, lead in plan:
            if t - lead >= 0:
                stage(t - lead)

    def step(t, carry):
        for stage, lead in plan:
            h = t - lead

            @pl.when(jnp.logical_and(h >= 0, h < KEY_HEADS))
            def _():
                stage(h)

        return carry

    below = lax.broadcasted_iota(jnp.int32, (SPAN, SPAN), 0)
    across = lax.broadcasted_iota(jnp.int32, (SPAN, SPAN), 1)
    for slot, (d_out, d_in) in enumerate(((0, 0), (1, 0), (0, 1), (0, 2), (1, 1), (1, 2))):
        block = ((o + 16 - d_out) % 16) * 16 + (i + 16 - d_in) % 16
        for s in range(2):
            key_at = order[block * 2 + s] * SPAN
            for r in range(2):
                query_at = order[(o * 16 + i) * 2 + r] * SPAN
                seen = key_at + across <= query_at + below
                bias[r * SPAN:(r + 1) * SPAN, (slot * 2 + s) * SPAN:(slot * 2 + s + 1) * SPAN] = (
                    jnp.where(seen, 0.0, -jnp.inf)
                )

    lax.fori_loop(0, end, step, 0)

    def finish(h, carry):
        out_copy(h).wait()
        for flow in (F_IN1, F_OUT0, F_OUT1, F_OUT2):
            left(h, flow)
        for at in range(4):
            @pl.when(x == at)
            def _():
                left(h, F_DOWN, UP[at], BOTH)

            @pl.when(source_x == at)
            def _():
                left(h, F_DOWN2, UP[at], BOTH)

            @pl.when(down_x == at)
            def _():
                left(h, F_UP2, 0, UP[at])

        @pl.when(x == 0)
        def _():
            left(h, F_WRAP, 0, FIRST)

        @pl.when(turns_y)
        def _():
            left(h, F_YWRAP)

        return carry

    lax.fori_loop(0, KEY_HEADS, finish, 0)


def shards(queries, key_codes, value_code_rows, key_scales, value_scales, formats, span_order):
    smem = pl.BlockSpec(memory_space=pltpu.SMEM)
    anywhere = pl.BlockSpec(memory_space=pl.ANY)
    flops = 4 * 32 * ROWS * SLOTS * ROWS * SIZE
    return pl.pallas_call(
        kernel,
        out_shape=pltpu.VMEM((ROWS, KEY_HEADS * GROUP * SIZE), jnp.bfloat16),
        in_specs=[smem, smem, smem, smem, anywhere, anywhere, anywhere],
        out_specs=anywhere,
        scratch_shapes=[
            pltpu.VMEM((KEY_HEADS, 9, BOTH, SIZE), jnp.bfloat16),
            pltpu.VMEM((ROWS, SLOTS * ROWS), jnp.float32),
            pltpu.VMEM((KEY_HEADS, GROUP, ROWS, SIZE), jnp.float32),
            pltpu.VMEM((KEY_HEADS, GROUP, ROWS, SIZE), jnp.float32),
            pltpu.VMEM((KEY_HEADS, GROUP, ROWS, SIZE), jnp.float32),
            pltpu.VMEM((ROWS, KEY_HEADS * SIZE), jnp.bfloat16),
            pltpu.VMEM((ROWS, KEY_HEADS * SIZE), jnp.bfloat16),
            pltpu.VMEM((ROWS, KEY_HEADS * GROUP * SIZE), jnp.bfloat16),
            pltpu.VMEM((KEY_HEADS, ROWS, GROUP * SIZE), jnp.bfloat16),
            pltpu.SemaphoreType.DMA((KEY_HEADS, 9)),
            pltpu.SemaphoreType.DMA((KEY_HEADS, 9)),
            pltpu.SemaphoreType.DMA((3,)),
            pltpu.SemaphoreType.DMA((KEY_HEADS,)),
        ],
        compiler_params=pltpu.CompilerParams(
            collective_id=1, has_side_effects=True, vmem_limit_bytes=60 * 2**20
        ),
        cost_estimate=pl.CostEstimate(
            flops=flops, bytes_accessed=6 * 2**20, transcendentals=32 * ROWS * SLOTS * ROWS
        ),
        name="block_window_attention",
    )(key_scales, value_scales, formats, span_order, key_codes, value_code_rows, queries)


def solution(mesh):
    split = P(("outer", "inner"), None)
    return jax.shard_map(
        shards,
        mesh=mesh,
        in_specs=(split, split, split, split, split, P(), P()),
        out_specs=split,
        check_vma=False,
    )
```

```python
import math

import jax
import jax.numpy as jnp
from jax import lax
from jax.experimental import pallas as pl
from jax.experimental.pallas import tpu as pltpu
from jax.sharding import PartitionSpec as P

MESH = pl.DeviceIdType.MESH
KEY_HEADS = 8
GROUP = 4
SIZE = 128
SPAN = 128
ROWS = 256
SLOTS = 6
HALF = 3
EXP_SCALE = math.log2(math.e) / math.sqrt(SIZE)

OWN, OUT0, IN1, IN2, OUT1, OUT2, VIA_Z, VIA_X, VIA_Y, VIA_Y2 = range(10)
LATE_Y = 10
F_IN1, F_DOWN, F_OUT0, F_WRAP, F_DOWN2, F_UP2, F_OUT1, F_OUT2, F_YWRAP, F_YWRAP2 = range(10)

UP = (128, 256, 80, 304)
HIGH = 400
FIRST = 304
BOTH = 2 * ROWS
QUARTER = 128
MOST = 384


def plan_of(
    send_via, send_in, send_out, relay_wrap, relay_down, relay_in1, relay_in2,
    relay_y0, relay_y1, relay_y, relay_y2, attend_near, attend_far
):
    return (
        (send_via, -2),
        (send_in, -2),
        (relay_wrap, 1),
        (relay_down, 1),
        (relay_y0, 1),
        (relay_in1, 2),
        (relay_in2, 3),
        (relay_y, 3),
        (relay_y1, 2),
        (relay_y2, 4),
        (send_out, -1),
        (attend_near(range(GROUP)), 3),
        (attend_far(range(GROUP)), 4),
    )


def kernel(
    kscale, vscale, formats, order, k_hbm, v_hbm, q_hbm, out_hbm,
    kv, bias, sums, peaks, totals, k_ref, v_ref, q_ref, o_ref, recv, sent, in_sem, o_sem,
):
    o = lax.axis_index("outer")
    i = lax.axis_index("inner")
    c = o % 2
    y = (o // 2) % 4
    x = i % 4
    zh = i // 4

    next_in = (i + 1) % 16
    next_out = (o + 1) % 16
    source_x = (x + 1) % 4
    down_x = (x + 3) % 4
    down_to = zh * 4 + down_x
    down2_to = (zh * 4 + source_x + 2) % 16
    z_lo = o // 8
    wraps_y = jnp.logical_and(y == 3, c == 1)
    turns_y = jnp.logical_and(y < 3, c == 1)
    turns_at = [jnp.logical_and(y == at, c == 1) for at in range(3)]
    past_wrap = 8 - 8 * z_lo

    k_copy = pltpu.make_async_copy(k_hbm, k_ref, in_sem.at[0])
    v_copy = pltpu.make_async_copy(v_hbm, v_ref, in_sem.at[1])
    q_copy = pltpu.make_async_copy(q_hbm, q_ref, in_sem.at[2])
    k_copy.start()
    v_copy.start()
    q_copy.start()

    barrier = pltpu.get_barrier_semaphore()

    def greet(outer, inner):
        pl.semaphore_signal(barrier, inc=1, device_id=(outer, inner), device_id_type=MESH)

    greet(o, (i + 15) % 16)
    greet(o, zh * 4 + (x + 1) % 4)
    two_back = (i + 14) % 16
    greet(o, (two_back // 4) * 4 + (x + 1) % 4)
    greet((o + 15) % 16, i)

    @pl.when(x == 0)
    def _():
        greet(o, i + 3)
        greet(o, (i + 12) % 16)

    @pl.when(x == 1)
    def _():
        greet(o, (i + 13) % 16)

    @pl.when(turns_y)
    def _():
        greet(z_lo * 8 + 7, i)

    @pl.when(jnp.logical_and(y == 0, c == 0))
    def _():
        greet(past_wrap + 1, i)
        greet(past_wrap + 3, i)
        greet(z_lo * 8 + 3, i)

    @pl.when(turns_at[1])
    def _():
        greet(past_wrap + 5, i)

    for which, codes, scale, copy in ((0, k_ref, kscale, k_copy), (1, v_ref, vscale, v_copy)):
        copy.wait()
        for h in range(KEY_HEADS):
            unit = jnp.where(formats[which, h] == 0, 1.0, 0.25)
            for s in range(2):
                part = codes[s * SPAN:(s + 1) * SPAN, h * SIZE:(h + 1) * SIZE].astype(jnp.float32)
                start = which * ROWS + s * SPAN
                kv[h, OWN, start:start + SPAN] = (part * (scale[s, h] * unit)).astype(jnp.bfloat16)

    peers = (
        4
        + jnp.where(jnp.logical_or(x == 0, x == 3), 1, 0)
        + jnp.where(turns_y, 1, 0)
        + jnp.where(turns_at[1], 1, 0)
        + jnp.where(x == 2, 1, 0)
        + jnp.where(wraps_y, 3, 0)
    )
    pl.semaphore_wait(barrier, peers)

    def send(h, source, target, flow, device, start=0, stop=BOTH, signal=None):
        rows = pl.ds(start, stop - start)
        pltpu.make_async_remote_copy(
            kv.at[h, source, rows], kv.at[h, target, rows], sent.at[h, flow],
            recv.at[h, target if signal is None else signal],
            device_id=device, device_id_type=MESH,
        ).start()

    def arrived(h, slot, start=0, stop=BOTH, signal=None):
        rows = pl.ds(start, stop - start)
        pltpu.make_async_copy(
            kv.at[h, slot, rows], kv.at[h, slot, rows],
            recv.at[h, slot if signal is None else signal],
        ).wait()

    def left(h, flow, start=0, stop=BOTH):
        rows = pl.ds(start, stop - start)
        pltpu.make_async_copy(kv.at[h, OWN, rows], kv.at[h, OWN, rows], sent.at[h, flow]).wait()

    def send_via(h):
        @pl.when(x == 3)
        def _():
            send(h, OWN, VIA_Z, F_IN1, (o, i - 3), 0, FIRST)

        for at in range(4):
            @pl.when(x == at)
            def _():
                stop = HIGH if at == 2 else BOTH
                if at == 2:
                    send(h, OWN, VIA_X, F_DOWN, (o, (i + 3) % 16), HIGH, BOTH)
                send(h, OWN, VIA_X, F_DOWN, (o, down_to), UP[at], stop)

    def send_in(h):
        @pl.when(x == 3)
        def _():
            send(h, OWN, IN1, F_IN1, (o, next_in), FIRST, BOTH)

        @pl.when(x != 3)
        def _():
            send(h, OWN, IN1, F_IN1, (o, next_in))

    def send_out(h):
        @pl.when(wraps_y)
        def _():
            send(h, OWN, VIA_Y, F_OUT0, (z_lo * 8 + 5, i), QUARTER, BOTH)
            send(h, OWN, VIA_Y, F_OUT0, (z_lo * 8 + 3, i), 0, QUARTER)

        @pl.when(jnp.logical_not(wraps_y))
        def _():
            send(h, OWN, OUT0, F_OUT0, (next_out, i))

    def relay_wrap(h):
        @pl.when(x == 0)
        def _():
            arrived(h, VIA_Z, 0, FIRST)
            send(h, VIA_Z, IN1, F_WRAP, (o, (i + 4) % 16), 0, FIRST)

    def relay_down(h):
        for at in range(4):
            @pl.when(source_x == at)
            def _():
                stop = HIGH if at == 2 else BOTH
                arrived(h, VIA_X, UP[at], BOTH)
                send(h, VIA_X, IN2, F_DOWN2, (o, down2_to), UP[at], stop)
                if at == 2:
                    send(h, VIA_X, IN2, F_DOWN2, (o, i - 1), HIGH, BOTH)

    def relay_in1(h):
        arrived(h, IN1)
        for at in range(4):
            @pl.when(down_x == at)
            def _():
                send(h, IN1, IN2, F_UP2, (o, next_in), 0, UP[at])

        @pl.when(wraps_y)
        def _():
            send(h, IN1, VIA_Y, F_OUT1, (z_lo * 8 + 1, i), 0, ROWS)
            send(h, IN1, VIA_Y, F_OUT1, (z_lo * 8 + 3, i), ROWS, BOTH, LATE_Y)

        @pl.when(jnp.logical_not(wraps_y))
        def _():
            send(h, IN1, OUT1, F_OUT1, (next_out, i))

    def relay_in2(h):
        arrived(h, IN2)

        @pl.when(wraps_y)
        def _():
            send(h, IN2, VIA_Y, F_OUT2, (z_lo * 8 + 1, i), MOST, BOTH, LATE_Y)
            send(h, IN2, OUT2, F_OUT2, (past_wrap, i), 0, MOST)

        @pl.when(jnp.logical_not(wraps_y))
        def _():
            send(h, IN2, OUT2, F_OUT2, (next_out, i))

    def relay_y0(h):
        @pl.when(turns_at[1])
        def _():
            arrived(h, VIA_Y, 0, QUARTER)
            send(h, VIA_Y, OUT0, F_YWRAP, (past_wrap, i), 0, QUARTER)

        @pl.when(turns_at[2])
        def _():
            arrived(h, VIA_Y, QUARTER, BOTH)
            send(h, VIA_Y, VIA_Y2, F_YWRAP, (past_wrap + 3, i), QUARTER, BOTH)

    def relay_y1(h):
        @pl.when(turns_at[1])
        def _():
            arrived(h, VIA_Y2, QUARTER, BOTH)
            send(h, VIA_Y2, OUT0, F_YWRAP2, (z_lo * 8, i), QUARTER, BOTH)

    def relay_y(h):
        @pl.when(turns_at[0])
        def _():
            arrived(h, VIA_Y, 0, ROWS)
            send(h, VIA_Y, OUT1, F_YWRAP, (past_wrap, i), 0, ROWS)

        @pl.when(turns_at[1])
        def _():
            arrived(h, VIA_Y, ROWS, BOTH, LATE_Y)
            send(h, VIA_Y, OUT1, F_YWRAP, (past_wrap, i), ROWS, BOTH)

    def relay_y2(h):
        @pl.when(turns_at[0])
        def _():
            arrived(h, VIA_Y, MOST, BOTH, LATE_Y)
            send(h, VIA_Y, OUT2, F_YWRAP, (past_wrap, i), MOST, BOTH)

    def out_copy(h):
        return pltpu.make_async_copy(
            o_ref.at[h],
            out_hbm.at[:, pl.ds(pl.multiple_of(h * (GROUP * SIZE), GROUP * SIZE), GROUP * SIZE)],
            o_sem.at[h],
        )

    def scores(h, g, first):
        columns = pl.ds(pl.multiple_of((h * GROUP + g) * SIZE, SIZE), SIZE)
        keys = kv[h, first:first + HALF, 0:ROWS].reshape(HALF * ROWS, SIZE)
        return lax.dot_general(
            q_ref[:, columns], keys, (((1,), (1,)), ((), ())),
            preferred_element_type=jnp.float32,
        ) + bias[:, first * ROWS:(first + HALF) * ROWS]

    def weighted(h, score, peak, first):
        expo = jnp.exp2((score - peak) * EXP_SCALE)
        values = kv[h, first:first + HALF, ROWS:BOTH].reshape(HALF * ROWS, SIZE)
        values = jnp.concatenate([values, jnp.ones((HALF * ROWS, SIZE), jnp.bfloat16)], axis=1)
        summed = jnp.dot(expo.astype(jnp.bfloat16), values, preferred_element_type=jnp.float32)
        return summed[:, :SIZE], summed[:, SIZE:]

    def attend_near(gs):
        def run(h):
            arrived(h, OUT0)

            @pl.when(h == 0)
            def _():
                q_copy.wait()

            for g in gs:
                score = scores(h, g, 0)
                peak = jnp.max(score, axis=1, keepdims=True)
                summed, total = weighted(h, score, peak, 0)
                sums[h, g] = summed
                peaks[h, g] = jnp.broadcast_to(peak, (ROWS, SIZE))
                totals[h, g] = total

        return run

    def attend_far(gs):
        def run(h):
            arrived(h, OUT1)
            arrived(h, OUT2)
            for g in gs:
                score = scores(h, g, HALF)
                near = peaks[h, g][:, 0:1]
                peak = jnp.maximum(near, jnp.max(score, axis=1, keepdims=True))
                summed, total = weighted(h, score, peak, HALF)
                keep = jnp.exp2((near - peak) * EXP_SCALE)
                result = (sums[h, g] * keep + summed) / (totals[h, g] * keep + total)
                o_ref[h, :, g * SIZE:(g + 1) * SIZE] = result.astype(jnp.bfloat16)
            out_copy(h).start()

        return run

    plan = plan_of(
        send_via, send_in, send_out, relay_wrap, relay_down, relay_in1, relay_in2, relay_y0, relay_y1, relay_y, relay_y2,
        attend_near, attend_far,
    )
    end = KEY_HEADS + max(lead for _, lead in plan)
    for t in range(min(lead for _, lead in plan), 0):
        for stage, lead in plan:
            if t - lead >= 0:
                stage(t - lead)

    def step(t, carry):
        for stage, lead in plan:
            h = t - lead

            @pl.when(jnp.logical_and(h >= 0, h < KEY_HEADS))
            def _():
                stage(h)

        return carry

    below = lax.broadcasted_iota(jnp.int32, (SPAN, SPAN), 0)
    across = lax.broadcasted_iota(jnp.int32, (SPAN, SPAN), 1)
    for slot, (d_out, d_in) in enumerate(((0, 0), (1, 0), (0, 1), (0, 2), (1, 1), (1, 2))):
        block = ((o + 16 - d_out) % 16) * 16 + (i + 16 - d_in) % 16
        for s in range(2):
            key_at = order[block * 2 + s] * SPAN
            for r in range(2):
                query_at = order[(o * 16 + i) * 2 + r] * SPAN
                seen = key_at + across <= query_at + below
                bias[r * SPAN:(r + 1) * SPAN, (slot * 2 + s) * SPAN:(slot * 2 + s + 1) * SPAN] = (
                    jnp.where(seen, 0.0, -jnp.inf)
                )

    lax.fori_loop(0, end, step, 0)

    def finish(h, carry):
        out_copy(h).wait()
        for flow in (F_IN1, F_OUT0, F_OUT1, F_OUT2):
            left(h, flow)
        for at in range(4):
            @pl.when(x == at)
            def _():
                left(h, F_DOWN, UP[at], BOTH)

            @pl.when(source_x == at)
            def _():
                left(h, F_DOWN2, UP[at], BOTH)

            @pl.when(down_x == at)
            def _():
                left(h, F_UP2, 0, UP[at])

        @pl.when(x == 0)
        def _():
            left(h, F_WRAP, 0, FIRST)

        @pl.when(turns_y)
        def _():
            left(h, F_YWRAP, 0, MOST)

        @pl.when(turns_at[1])
        def _():
            left(h, F_YWRAP2, 0, MOST)

        return carry

    lax.fori_loop(0, KEY_HEADS, finish, 0)


def shards(queries, key_codes, value_code_rows, key_scales, value_scales, formats, span_order):
    smem = pl.BlockSpec(memory_space=pltpu.SMEM)
    anywhere = pl.BlockSpec(memory_space=pl.ANY)
    flops = 4 * 32 * ROWS * SLOTS * ROWS * SIZE
    return pl.pallas_call(
        kernel,
        out_shape=pltpu.VMEM((ROWS, KEY_HEADS * GROUP * SIZE), jnp.bfloat16),
        in_specs=[smem, smem, smem, smem, anywhere, anywhere, anywhere],
        out_specs=anywhere,
        scratch_shapes=[
            pltpu.VMEM((KEY_HEADS, 10, BOTH, SIZE), jnp.bfloat16),
            pltpu.VMEM((ROWS, SLOTS * ROWS), jnp.float32),
            pltpu.VMEM((KEY_HEADS, GROUP, ROWS, SIZE), jnp.float32),
            pltpu.VMEM((KEY_HEADS, GROUP, ROWS, SIZE), jnp.float32),
            pltpu.VMEM((KEY_HEADS, GROUP, ROWS, SIZE), jnp.float32),
            pltpu.VMEM((ROWS, KEY_HEADS * SIZE), jnp.bfloat16),
            pltpu.VMEM((ROWS, KEY_HEADS * SIZE), jnp.bfloat16),
            pltpu.VMEM((ROWS, KEY_HEADS * GROUP * SIZE), jnp.bfloat16),
            pltpu.VMEM((KEY_HEADS, ROWS, GROUP * SIZE), jnp.bfloat16),
            pltpu.SemaphoreType.DMA((KEY_HEADS, 11)),
            pltpu.SemaphoreType.DMA((KEY_HEADS, 10)),
            pltpu.SemaphoreType.DMA((3,)),
            pltpu.SemaphoreType.DMA((KEY_HEADS,)),
        ],
        compiler_params=pltpu.CompilerParams(
            collective_id=1, has_side_effects=True, vmem_limit_bytes=60 * 2**20
        ),
        cost_estimate=pl.CostEstimate(
            flops=flops, bytes_accessed=6 * 2**20, transcendentals=32 * ROWS * SLOTS * ROWS
        ),
        name="block_window_attention",
    )(key_scales, value_scales, formats, span_order, key_codes, value_code_rows, queries)


def solution(mesh):
    split = P(("outer", "inner"), None)
    return jax.shard_map(
        shards,
        mesh=mesh,
        in_specs=(split, split, split, split, split, P(), P()),
        out_specs=split,
        check_vma=False,
    )
```

```python
import math

import jax
import jax.numpy as jnp
from jax import lax
from jax.experimental import pallas as pl
from jax.experimental.pallas import tpu as pltpu
from jax.sharding import PartitionSpec as P

MESH = pl.DeviceIdType.MESH
KEY_HEADS = 8
GROUP = 4
SIZE = 128
SPAN = 128
ROWS = 256
SLOTS = 6
HALF = 3
EXP_SCALE = math.log2(math.e) / math.sqrt(SIZE)

OWN, OUT0, IN1, IN2, OUT1, OUT2, VIA_Z, VIA_X, VIA_Y = range(9)
F_IN1, F_DOWN, F_OUT0, F_WRAP, F_DOWN2, F_UP2, F_OUT1, F_OUT2, F_YWRAP = range(9)

FIRST_SENT = 2
UP = (128, 256, 80, 352)
HIGH = 384
FIRST = 304
BOTH = 2 * ROWS


def plan_of(
    send_via, send_in, send_out, relay_wrap, relay_down, relay_in1, relay_in2, relay_y0, relay_y,
    attend_near, attend_far, finish
):
    return (
        (send_via, -2),
        (send_in, -2),
        (relay_wrap, 1),
        (relay_down, 1),
        (relay_y0, 1),
        (relay_in1, 2),
        (relay_in2, 3),
        (relay_y, 3),
        (send_out, -1),
        (attend_near(range(GROUP)), 3),
        (attend_far(range(GROUP)), 4),
        (finish, 5),
    )


def kernel(
    kscale, vscale, formats, order, k_hbm, v_hbm, q_hbm, out_hbm,
    kv, bias, sums, peaks, totals, k_ref, v_ref, q_ref, o_ref, recv, sent, in_sem, o_sem,
):
    o = lax.axis_index("outer")
    i = lax.axis_index("inner")
    c = o % 2
    y = (o // 2) % 4
    x = i % 4
    zh = i // 4

    next_in = (i + 1) % 16
    next_out = (o + 1) % 16
    source_x = (x + 1) % 4
    down_x = (x + 3) % 4
    down_to = zh * 4 + down_x
    down2_to = (zh * 4 + source_x + 2) % 16
    z_lo = o // 8
    wraps_y = jnp.logical_and(y == 3, c == 1)
    turns_y = jnp.logical_and(y < 2, c == 1)
    past_wrap = 8 - 8 * z_lo

    k_copy = pltpu.make_async_copy(k_hbm, k_ref, in_sem.at[0])
    v_copy = pltpu.make_async_copy(v_hbm, v_ref, in_sem.at[1])
    q_copy = pltpu.make_async_copy(q_hbm, q_ref, in_sem.at[2])
    k_copy.start()
    v_copy.start()
    q_copy.start()

    barrier = pltpu.get_barrier_semaphore()

    def greet(outer, inner):
        pl.semaphore_signal(barrier, inc=1, device_id=(outer, inner), device_id_type=MESH)

    greet(o, (i + 15) % 16)
    greet(o, zh * 4 + (x + 1) % 4)
    two_back = (i + 14) % 16
    greet(o, (two_back // 4) * 4 + (x + 1) % 4)
    greet((o + 15) % 16, i)

    @pl.when(x == 0)
    def _():
        greet(o, i + 3)
        greet(o, (i + 12) % 16)

    @pl.when(x == 1)
    def _():
        greet(o, (i + 13) % 16)

    @pl.when(turns_y)
    def _():
        greet(z_lo * 8 + 7, i)

    @pl.when(jnp.logical_and(y == 0, c == 0))
    def _():
        greet(past_wrap + 1, i)
        greet(past_wrap + 3, i)

    def dequantize(h):
        for which, codes, scale in ((0, k_ref, kscale), (1, v_ref, vscale)):
            unit = jnp.where(formats[which, h] == 0, 1.0, 0.25)
            for s in range(2):
                part = codes[s * SPAN:(s + 1) * SPAN, h * SIZE:(h + 1) * SIZE].astype(jnp.float32)
                start = which * ROWS + s * SPAN
                kv[h, OWN, start:start + SPAN] = (part * (scale[s, h] * unit)).astype(jnp.bfloat16)

    k_copy.wait()
    v_copy.wait()
    for h in range(FIRST_SENT):
        dequantize(h)

    peers = (
        4
        + jnp.where(jnp.logical_or(x == 0, x == 3), 1, 0)
        + jnp.where(turns_y, 1, 0)
        + jnp.where(x == 2, 1, 0)
        + jnp.where(wraps_y, 2, 0)
    )
    pl.semaphore_wait(barrier, peers)

    def send(h, source, target, flow, device, start=0, stop=BOTH):
        rows = pl.ds(start, stop - start)
        pltpu.make_async_remote_copy(
            kv.at[h, source, rows], kv.at[h, target, rows], sent.at[h, flow], recv.at[h, target],
            device_id=device, device_id_type=MESH,
        ).start()

    def arrived(h, slot, start=0, stop=BOTH):
        rows = pl.ds(start, stop - start)
        pltpu.make_async_copy(kv.at[h, slot, rows], kv.at[h, slot, rows], recv.at[h, slot]).wait()

    def left(h, flow, start=0, stop=BOTH):
        rows = pl.ds(start, stop - start)
        pltpu.make_async_copy(kv.at[h, OWN, rows], kv.at[h, OWN, rows], sent.at[h, flow]).wait()

    def send_via(h):
        @pl.when(x == 3)
        def _():
            send(h, OWN, VIA_Z, F_IN1, (o, i - 3), 0, FIRST)

        for at in range(4):
            @pl.when(x == at)
            def _():
                stop = HIGH if at == 2 else BOTH
                if at == 2:
                    send(h, OWN, VIA_X, F_DOWN, (o, (i + 3) % 16), HIGH, BOTH)
                send(h, OWN, VIA_X, F_DOWN, (o, down_to), UP[at], stop)

    def send_in(h):
        @pl.when(x == 3)
        def _():
            send(h, OWN, IN1, F_IN1, (o, next_in), FIRST, BOTH)

        @pl.when(x != 3)
        def _():
            send(h, OWN, IN1, F_IN1, (o, next_in))

    def send_out(h):
        @pl.when(wraps_y)
        def _():
            send(h, OWN, VIA_Y, F_OUT0, (z_lo * 8 + 3, i))

        @pl.when(jnp.logical_not(wraps_y))
        def _():
            send(h, OWN, OUT0, F_OUT0, (next_out, i))

    def relay_wrap(h):
        @pl.when(x == 0)
        def _():
            arrived(h, VIA_Z, 0, FIRST)
            send(h, VIA_Z, IN1, F_WRAP, (o, (i + 4) % 16), 0, FIRST)

    def relay_down(h):
        for at in range(4):
            @pl.when(source_x == at)
            def _():
                stop = HIGH if at == 2 else BOTH
                arrived(h, VIA_X, UP[at], BOTH)
                send(h, VIA_X, IN2, F_DOWN2, (o, down2_to), UP[at], stop)
                if at == 2:
                    send(h, VIA_X, IN2, F_DOWN2, (o, i - 1), HIGH, BOTH)

    def relay_in1(h):
        arrived(h, IN1)
        for at in range(4):
            @pl.when(down_x == at)
            def _():
                send(h, IN1, IN2, F_UP2, (o, next_in), 0, UP[at])

        @pl.when(wraps_y)
        def _():
            send(h, IN1, VIA_Y, F_OUT1, (z_lo * 8 + 1, i))

        @pl.when(jnp.logical_not(wraps_y))
        def _():
            send(h, IN1, OUT1, F_OUT1, (next_out, i))

    def relay_in2(h):
        arrived(h, IN2)
        send(h, IN2, OUT2, F_OUT2, (next_out, i))

    def relay_y(h):
        @pl.when(jnp.logical_and(y == 0, c == 1))
        def _():
            arrived(h, VIA_Y)
            send(h, VIA_Y, OUT1, F_YWRAP, (past_wrap, i))

    def relay_y0(h):
        @pl.when(jnp.logical_and(y == 1, c == 1))
        def _():
            arrived(h, VIA_Y)
            send(h, VIA_Y, OUT0, F_YWRAP, (past_wrap, i))

    def out_copy(h):
        return pltpu.make_async_copy(
            o_ref.at[h],
            out_hbm.at[:, pl.ds(pl.multiple_of(h * (GROUP * SIZE), GROUP * SIZE), GROUP * SIZE)],
            o_sem.at[h],
        )

    def scores(h, g, first):
        columns = pl.ds(pl.multiple_of((h * GROUP + g) * SIZE, SIZE), SIZE)
        keys = kv[h, first:first + HALF, 0:ROWS].reshape(HALF * ROWS, SIZE)
        return lax.dot_general(
            q_ref[:, columns], keys, (((1,), (1,)), ((), ())),
            preferred_element_type=jnp.float32,
        ) + bias[:, first * ROWS:(first + HALF) * ROWS]

    def weighted(h, score, peak, first):
        expo = jnp.exp2((score - peak) * EXP_SCALE)
        values = kv[h, first:first + HALF, ROWS:BOTH].reshape(HALF * ROWS, SIZE)
        values = jnp.concatenate([values, jnp.ones((HALF * ROWS, SIZE), jnp.bfloat16)], axis=1)
        summed = jnp.dot(expo.astype(jnp.bfloat16), values, preferred_element_type=jnp.float32)
        return summed[:, :SIZE], summed[:, SIZE:]

    def attend_near(gs):
        def run(h):
            arrived(h, OUT0)

            @pl.when(h == 0)
            def _():
                q_copy.wait()

            for g in gs:
                score = scores(h, g, 0)
                peak = jnp.max(score, axis=1, keepdims=True)
                summed, total = weighted(h, score, peak, 0)
                sums[h, g] = summed
                peaks[h, g] = jnp.broadcast_to(peak, (ROWS, SIZE))
                totals[h, g] = total

        return run

    def attend_far(gs):
        def run(h):
            arrived(h, OUT1)
            arrived(h, OUT2)
            for g in gs:
                score = scores(h, g, HALF)
                near = peaks[h, g][:, 0:1]
                peak = jnp.maximum(near, jnp.max(score, axis=1, keepdims=True))
                summed, total = weighted(h, score, peak, HALF)
                keep = jnp.exp2((near - peak) * EXP_SCALE)
                result = (sums[h, g] * keep + summed) / (totals[h, g] * keep + total)
                o_ref[h, :, g * SIZE:(g + 1) * SIZE] = result.astype(jnp.bfloat16)
            out_copy(h).start()

        return run

    def finish(h):
        out_copy(h).wait()
        for flow in (F_IN1, F_OUT0, F_OUT1, F_OUT2):
            left(h, flow)
        for at in range(4):
            @pl.when(x == at)
            def _():
                left(h, F_DOWN, UP[at], BOTH)

            @pl.when(source_x == at)
            def _():
                left(h, F_DOWN2, UP[at], BOTH)

            @pl.when(down_x == at)
            def _():
                left(h, F_UP2, 0, UP[at])

        @pl.when(x == 0)
        def _():
            left(h, F_WRAP, 0, FIRST)

        @pl.when(turns_y)
        def _():
            left(h, F_YWRAP)

    plan = plan_of(
        send_via, send_in, send_out, relay_wrap, relay_down, relay_in1, relay_in2, relay_y0, relay_y,
        attend_near, attend_far, finish,
    )
    end = KEY_HEADS + max(lead for _, lead in plan)
    for t in range(min(lead for _, lead in plan), 0):
        for stage, lead in plan:
            if t - lead >= 0:
                stage(t - lead)

    for h in range(FIRST_SENT, KEY_HEADS):
        dequantize(h)

    def step(t, carry):
        for stage, lead in plan:
            h = t - lead

            @pl.when(jnp.logical_and(h >= 0, h < KEY_HEADS))
            def _():
                stage(h)

        return carry

    below = lax.broadcasted_iota(jnp.int32, (SPAN, SPAN), 0)
    across = lax.broadcasted_iota(jnp.int32, (SPAN, SPAN), 1)
    for slot, (d_out, d_in) in enumerate(((0, 0), (1, 0), (0, 1), (0, 2), (1, 1), (1, 2))):
        block = ((o + 16 - d_out) % 16) * 16 + (i + 16 - d_in) % 16
        for s in range(2):
            key_at = order[block * 2 + s] * SPAN
            for r in range(2):
                query_at = order[(o * 16 + i) * 2 + r] * SPAN
                seen = key_at + across <= query_at + below
                bias[r * SPAN:(r + 1) * SPAN, (slot * 2 + s) * SPAN:(slot * 2 + s + 1) * SPAN] = (
                    jnp.where(seen, 0.0, -jnp.inf)
                )

    lax.fori_loop(0, end, step, 0)


def shards(queries, key_codes, value_code_rows, key_scales, value_scales, formats, span_order):
    smem = pl.BlockSpec(memory_space=pltpu.SMEM)
    anywhere = pl.BlockSpec(memory_space=pl.ANY)
    flops = 4 * 32 * ROWS * SLOTS * ROWS * SIZE
    return pl.pallas_call(
        kernel,
        out_shape=pltpu.VMEM((ROWS, KEY_HEADS * GROUP * SIZE), jnp.bfloat16),
        in_specs=[smem, smem, smem, smem, anywhere, anywhere, anywhere],
        out_specs=anywhere,
        scratch_shapes=[
            pltpu.VMEM((KEY_HEADS, 9, BOTH, SIZE), jnp.bfloat16),
            pltpu.VMEM((ROWS, SLOTS * ROWS), jnp.float32),
            pltpu.VMEM((KEY_HEADS, GROUP, ROWS, SIZE), jnp.float32),
            pltpu.VMEM((KEY_HEADS, GROUP, ROWS, SIZE), jnp.float32),
            pltpu.VMEM((KEY_HEADS, GROUP, ROWS, SIZE), jnp.float32),
            pltpu.VMEM((ROWS, KEY_HEADS * SIZE), jnp.bfloat16),
            pltpu.VMEM((ROWS, KEY_HEADS * SIZE), jnp.bfloat16),
            pltpu.VMEM((ROWS, KEY_HEADS * GROUP * SIZE), jnp.bfloat16),
            pltpu.VMEM((KEY_HEADS, ROWS, GROUP * SIZE), jnp.bfloat16),
            pltpu.SemaphoreType.DMA((KEY_HEADS, 9)),
            pltpu.SemaphoreType.DMA((KEY_HEADS, 9)),
            pltpu.SemaphoreType.DMA((3,)),
            pltpu.SemaphoreType.DMA((KEY_HEADS,)),
        ],
        compiler_params=pltpu.CompilerParams(
            collective_id=1, has_side_effects=True, vmem_limit_bytes=60 * 2**20
        ),
        cost_estimate=pl.CostEstimate(
            flops=flops, bytes_accessed=6 * 2**20, transcendentals=32 * ROWS * SLOTS * ROWS
        ),
        name="block_window_attention",
    )(key_scales, value_scales, formats, span_order, key_codes, value_code_rows, queries)


def solution(mesh):
    split = P(("outer", "inner"), None)
    return jax.shard_map(
        shards,
        mesh=mesh,
        in_specs=(split, split, split, split, split, P(), P()),
        out_specs=split,
        check_vma=False,
    )
```
